512 devices in a mesh: site: 64 (over y, x, core), term: 8 (over z).
Axes of the slice: x: 4, y: 8, z: 8, core: 2. Of those that a mesh axis runs over, the one named last changes fastest.
Arguments:
- left_env: float32 [64, 16, 8, 128, 128], P('site', 'term'), may hold values from -0.5 to 0.5
- right_env: float32 [64, 16, 8, 128, 128], P('site', 'term'), may hold values from -0.5 to 0.5
- transfer: float32 [64, 8, 128, 128], P('site'), may hold values from -1 to 2, as said below
- psi_start: float32 [64, 8, 128, 128], P('site'), may hold values from -6 to 6
- kept: int32 [64, 8], P('site'), may hold values from 64 to 128
Outputs:
- psi_out: float32 [64, 8, 128, 128], P('site')
- incoming_env: float32 [64, 16, 8, 128, 128], P('site', 'term')
The draws below stay inside these ranges and needn't reach their ends.
Inputs may be any that keep to these rules, and one draw needn't show every extreme that they name: `transfer`: the identity plus independent entries of deviation 0.2 / sqrt(128).
All inputs are finite; a program needn't handle non-finite values.
Results may differ from the reference program's by a relative error of at most 0.0003.
Values sent between devices are 32-bit elements; how exact they have to be, the bound alone decides.
No kernel may reach another device: no remote copies, remote signals or barrier semaphores. Data moves between devices by JAX's collectives and lax.ppermute only.
A program may use at most 128 MiB of HBM per device.

```python
import jax
import jax.numpy as jnp
from jax import lax

SB = 128
NSEC = 8
ITERS = 4
SEGMENTS = 64
TERMS = 16


def draw_transfer(key, part):
    key = jax.random.fold_in(key, 7)
    noise = jax.random.truncated_normal(key, -4.0, 4.0, (SEGMENTS, NSEC, SB, SB), jnp.float32)
    return jnp.eye(SB, dtype=jnp.float32) + 0.2 / SB ** 0.5 * noise


def plant(drawn, key, least, high):
    longest = drawn.shape.index(max(drawn.shape))
    spots = []
    for shift in (0, 1):
        where = [jax.random.randint(jax.random.fold_in(key, axis), (), 0, length) for axis, length in enumerate(drawn.shape)]
        where[longest] = (where[longest] + shift) % drawn.shape[longest]
        spots.append(tuple(where))
    return drawn.at[spots[0]].set(least).at[spots[1]].set(high)


def block_scale(stream_key, shape, pieces, low, top_value):
    def one(axis_at, parts):
        heights = jax.random.uniform(jax.random.fold_in(jax.random.fold_in(stream_key, 6), axis_at), (parts,), jnp.float32, low / len(pieces), top_value / len(pieces))
        return jnp.repeat(jnp.exp(heights), shape[axis_at] // parts).reshape((-1,) + (1,) * (len(shape) - axis_at - 1))

    loudness = one(*pieces[0])
    for cut in pieces[1:]:
        loudness = loudness * one(*cut)
    return loudness


def centred(stream_key, dims, width, bound, pieces=(), held_as=jnp.bfloat16):
    entries = width * jax.random.normal(stream_key, dims, jnp.float32)
    if pieces:
        entries = entries * block_scale(stream_key, dims, pieces, -0.22, 0.18)
    return jnp.clip(entries, -bound, bound).astype(held_as)


def setup_inputs(seed: int = 0) -> dict:
    seeds = jax.random.split(jax.random.key(seed), 6)
    left_env = centred(seeds[0], (SEGMENTS, TERMS, NSEC, SB, SB), SB ** -0.5, 0.5, ((0, 64), (1, 8)), jnp.float32)
    right_env = centred(seeds[1], (SEGMENTS, TERMS, NSEC, SB, SB), SB ** -0.5, 0.5, ((0, 64), (1, 8)), jnp.float32)
    transfer = draw_transfer(jax.random.fold_in(seeds[5], 71), 0)
    psi_start = centred(seeds[3], (SEGMENTS, NSEC, SB, SB), 1.0, 6.0, ((0, 64),), jnp.float32)
    kept = plant(jax.random.randint(seeds[4], (SEGMENTS, NSEC), SB // 2, SB + 1), jax.random.fold_in(seeds[4], 1), SB // 2, SB).astype(jnp.int32)
    return {"left_env": left_env, "right_env": right_env, "transfer": transfer, "psi_start": psi_start, "kept": kept}


highest = lax.Precision.HIGHEST
norm_eps = 1e-06
step_size = 0.5

def apply_terms(left_used, right_part, vector):
    partial_image = jnp.einsum('tsij,sjk->tsik', left_used, vector, precision=highest)
    return jnp.einsum('tsik,tskl->sil', partial_image, right_part, precision=highest)

def one_segment(packed):
    left_part, right_part, prefix, start, keep = packed
    left_used = jnp.einsum('sji,tsjk->tsik', prefix, left_part, precision=highest)
    left_used = jnp.einsum('tsik,skl->tsil', left_used, prefix, precision=highest)
    vector = start / jnp.sqrt(jnp.sum(start * start) + norm_eps)
    for step in range(ITERS):
        image = apply_terms(left_used, right_part, vector)
        energy = jnp.sum(vector * image)
        scale = jnp.sqrt(jnp.sum(image * image) + norm_eps)
        update = vector - step_size * (image - energy * vector) / scale
        vector = update / jnp.sqrt(jnp.sum(update * update) + norm_eps)
    columns = lax.broadcasted_iota(jnp.int32, vector.shape, 2)
    masked = jnp.where(columns < keep[:, None, None], vector, jnp.float32(0.0))
    result = masked / jnp.sqrt(jnp.sum(masked * masked) + norm_eps)
    boundary = jnp.einsum('sji,tsjk->tsik', result, left_used, precision=highest)
    boundary = jnp.einsum('tsik,skl->tsil', boundary, result, precision=highest)
    return (result, boundary)

def reference(left_env, right_env, transfer, psi_start, kept):
    identity_block = jnp.broadcast_to(jnp.eye(SB, dtype=jnp.float32), (NSEC, SB, SB))

    def advance(carry, matrix):
        return (jnp.einsum('sij,sjk->sik', carry, matrix, precision=highest), carry)
    last_prefix, prefixes = lax.scan(advance, identity_block, transfer)
    results, boundaries = lax.map(one_segment, (left_env, right_env, prefixes, psi_start, kept))
    incoming = jnp.concatenate([jnp.zeros_like(boundaries[:1]), boundaries[:-1]], axis=0)
    return (results, incoming)
```

```python
import functools

import jax
import jax.numpy as jnp
from jax import lax
from jax.experimental import pallas as pl
from jax.experimental.pallas import tpu as pltpu
from jax.sharding import Mesh, PartitionSpec as P

ITERS = 4
norm_eps = 1e-06
step_size = 0.5
SITE = ("y2", "y1", "y0", "x1", "x0", "c")
SCAN = ("c", "x0", "x1", "y0", "y1", "y2")
TERM = "z"
VMEM_LIMIT = 48 * 1024 * 1024


def halves(x):
    high = x.astype(jnp.bfloat16)
    low = (x - high.astype(jnp.float32)).astype(jnp.bfloat16)
    return high, low


def mm(a, b):
    return jnp.dot(a, b, preferred_element_type=jnp.float32)


def left_operand(a):
    return jnp.concatenate(halves(a), axis=1)


def right_operand(b):
    high, low = halves(b)
    top = jnp.concatenate([high, low], axis=1)
    bottom = jnp.concatenate([high, jnp.zeros_like(high)], axis=1)
    return jnp.concatenate([top, bottom], axis=0)


def joined(a, b):
    both = mm(a, right_operand(b))
    size = b.shape[1]
    return both[:, :size] + both[:, size:]


def total(x):
    return jnp.sum(jnp.sum(x, axis=0, keepdims=True), axis=1, keepdims=True)


def krylov_kernel(z_ref, blocks_ref, prefix_ref, start_ref, basis_ref, sent_ref, left_ref, right_ref):
    groups, per_group, size, _ = blocks_ref.shape
    own = per_group // 2
    terms = groups * own
    for group in range(groups):
        for term in range(own):
            at = (group * own + term) * size
            left_ref[at:at + size, :] = left_operand(blocks_ref[group, term])
            high, low = halves(blocks_ref[group, own + term])
            right_ref[at:at + size, :] = jnp.concatenate([high, low], axis=1)
    prefix = prefix_ref[...]
    forward = left_operand(prefix)
    backward = left_operand(prefix.T)
    squares = jnp.zeros((size, size), jnp.float32)
    for sector in range(start_ref.shape[0]):
        squares = squares + start_ref[sector] * start_ref[sector]
    x = start_ref[z_ref[0]] / jnp.sqrt(total(squares) + norm_eps)
    basis_ref[0] = x
    lane = lax.broadcasted_iota(jnp.int32, (1, size), 1)
    row = jnp.zeros((1, size), jnp.float32)
    basis = [x]
    for step in range(ITERS):
        w = joined(forward, x)
        middle = joined(left_ref[...], w)
        high, low = halves(middle)
        wide = jnp.concatenate(
            [
                jnp.concatenate([part[t * size:(t + 1) * size] for t in range(terms)], axis=1)
                for part in (high, low)
            ],
            axis=0,
        )
        both = mm(wide, right_ref[...])
        y = both[:size, :size] + (both[:size, size:] + both[size:, :size])
        y = joined(backward, y)
        length = jnp.sqrt(total(y * y))
        x = y / jnp.maximum(length, 1e-30)
        basis_ref[step + 1] = x
        basis.append(x)
        row = row + jnp.where(lane == step, length, 0.0)
    place = ITERS
    for i in range(ITERS + 1):
        for j in range(i, ITERS + 1):
            row = row + jnp.where(lane == place, total(basis[i] * basis[j]), 0.0)
            place += 1
    sheet = jnp.broadcast_to(row, (8, size))
    for target in range(groups):
        sent_ref[target, :size, :] = prefix
        sent_ref[target, size:, :] = sheet


def combine_kernel(z_ref, kept_ref, scalars_ref, basis_ref, sent_ref):
    table = scalars_ref[:, 0, :]
    sectors, size = table.shape

    def item(index):
        return table[:, index:index + 1]

    def over(x):
        return jnp.sum(x, axis=0, keepdims=True)

    rates = [jnp.ones((sectors, 1), jnp.float32)]
    ratio = []
    for j in range(ITERS):
        longer = rates[j] * item(j)
        largest = jnp.maximum(jnp.max(longer, axis=0, keepdims=True), 1e-30)
        ratio.append(largest)
        rates.append(longer / largest)
    gram = {}
    place = ITERS
    for i in range(ITERS + 1):
        for j in range(i, ITERS + 1):
            gram[i, j] = gram[j, i] = over(rates[i] * rates[j] * item(place))
            place += 1
    zero = jnp.zeros((1, 1), jnp.float32)
    vector = [jnp.ones((1, 1), jnp.float32)] + [zero] * ITERS

    def inner(a, b, upto_a, upto_b):
        out = zero
        for i in range(upto_a[0], upto_a[1] + 1):
            for j in range(upto_b[0], upto_b[1] + 1):
                out = out + a[i] * b[j] * gram[i, j]
        return out

    for step in range(ITERS):
        image = [zero] + [vector[j] * ratio[j] for j in range(ITERS)]
        energy = inner(vector, image, (0, step), (1, step + 1))
        scale = jnp.sqrt(inner(image, image, (1, step + 1), (1, step + 1)) + norm_eps)
        update = [vector[j] - step_size * (image[j] - energy * vector[j]) / scale for j in range(ITERS + 1)]
        length = jnp.sqrt(inner(update, update, (0, step + 1), (0, step + 1)) + norm_eps)
        vector = [part / length for part in update]

    mine = lax.broadcasted_iota(jnp.int32, (sectors, 1), 0) == z_ref[0]
    result = jnp.zeros((size, size), jnp.float32)
    for j in range(ITERS + 1):
        factor = over(jnp.where(mine, rates[j], 0.0)) * vector[j]
        result = result + factor * basis_ref[j]
    columns = lax.broadcasted_iota(jnp.int32, (size, size), 1)
    result = jnp.where(columns < kept_ref[0, z_ref[0]], result, 0.0)
    for target in range(sectors):
        sent_ref[target] = result


def finish_kernel(vector_ref, prefix_ref, psi_ref, moved_ref):
    sectors, size, _ = vector_ref.shape
    squares = jnp.zeros((size, size), jnp.float32)
    for sector in range(sectors):
        squares = squares + vector_ref[sector] * vector_ref[sector]
    length = jnp.sqrt(total(squares) + norm_eps)
    for sector in range(sectors):
        psi = vector_ref[sector] / length
        psi_ref[0, sector] = psi
        moved_ref[sector] = joined(left_operand(prefix_ref[sector, :size, :]), psi)


def boundary_kernel(moved_ref, left_ref, out_ref):
    own, sectors, size, _ = left_ref.shape
    for sector in range(sectors):
        u = moved_ref[sector]
        right = right_operand(u)
        across = left_operand(u.T)
        for term in range(own):
            half = mm(left_operand(left_ref[term, sector]), right)
            half = half[:, :size] + half[:, size:]
            out_ref[0, term, sector] = joined(across, half)


def vmem():
    return pl.BlockSpec(memory_space=pltpu.VMEM)


def smem():
    return pl.BlockSpec(memory_space=pltpu.SMEM)


def call(kernel, out_shape, in_specs, flops, scratch=()):
    return pl.pallas_call(
        kernel,
        out_shape=out_shape,
        in_specs=in_specs,
        out_specs=jax.tree.map(lambda _: vmem(), out_shape),
        scratch_shapes=scratch,
        compiler_params=pltpu.CompilerParams(vmem_limit_bytes=VMEM_LIMIT),
        cost_estimate=pl.CostEstimate(flops=flops, bytes_accessed=4 << 20, transcendentals=0),
    )


def struct(*shape):
    return jax.ShapeDtypeStruct(shape, jnp.float32)


def product(a, b):
    return jnp.dot(a, b, precision=lax.Precision.HIGHEST, preferred_element_type=jnp.float32)


def scanned(own):
    whole = own
    prefix = None
    for level, axis in enumerate(SCAN):
        with jax.named_scope("scan_" + axis):
            pair = lax.all_gather(whole, axis)
            upper = lax.axis_index(axis) == 1
            if prefix is None:
                prefix = jnp.where(upper, pair[0], jnp.eye(own.shape[0], dtype=own.dtype))
            else:
                prefix = jnp.where(upper, product(pair[0], prefix), prefix)
            if level + 1 < len(SCAN):
                whole = product(pair[0], pair[1])
    return prefix


def per_device(left_env, right_env, transfer, psi_start, kept):
    left, right, transfer, psi = left_env[0], right_env[0], transfer[0], psi_start[0]
    own, sectors, size, _ = left.shape
    z = lax.axis_index(TERM)
    spot = z[None]
    with jax.named_scope("gather_terms"):
        outgoing = jnp.concatenate([left, right], axis=0)
        blocks = lax.all_to_all(outgoing, TERM, 1, 0, tiled=False)
    with jax.named_scope("prefix"):
        prefix = scanned(lax.dynamic_index_in_dim(transfer, z, 0, keepdims=False))
    pairs = [(source, source + 1) for source in range(63)]
    with jax.named_scope("left_previous"):
        late, _ = lax.optimization_barrier((left, prefix))
        left_previous = lax.ppermute(late, SITE, pairs)
    with jax.named_scope("krylov"):
        terms = own * sectors
        basis, sent = call(
            krylov_kernel,
            (struct(ITERS + 1, size, size), struct(sectors, size + 8, size)),
            [smem(), vmem(), vmem(), vmem()],
            ITERS * terms * 4 * 2 * 3 * size**3,
            [pltpu.VMEM((terms * size, 2 * size), jnp.bfloat16)] * 2,
        )(spot, blocks, prefix, psi)
    with jax.named_scope("share_scalars"):
        shared = lax.all_to_all(sent, TERM, 0, 0, tiled=True)
    with jax.named_scope("combine"):
        scalars = shared[:, size:, :]
        sent = call(
            combine_kernel,
            struct(sectors, size, size),
            [smem(), smem(), vmem(), vmem()],
            size**2 * 100,
        )(spot, kept, scalars, basis)
    with jax.named_scope("share_psi"):
        vector = lax.all_to_all(sent, TERM, 0, 0, tiled=True)
    with jax.named_scope("finish"):
        result, moved = call(
            finish_kernel,
            (struct(1, sectors, size, size), struct(sectors, size, size)),
            [vmem(), vmem()],
            sectors * 6 * size**3,
        )(vector, shared)
    with jax.named_scope("hand_on"):
        moved = lax.ppermute(moved, SITE, pairs)
    with jax.named_scope("boundary"):
        incoming = call(
            boundary_kernel,
            struct(1, own, sectors, size, size),
            [vmem(), vmem()],
            own * sectors * 12 * size**3,
        )(moved, left_previous)
    return result, incoming


def solution(mesh):
    fine = Mesh(mesh.devices.reshape((2,) * 6 + (8,)), SITE + (TERM,))
    placed = (
        P(SITE, TERM, None, None, None),
        P(SITE, TERM, None, None, None),
        P(SITE, None, None, None),
        P(SITE, None, None, None),
        P(SITE, None),
    )
    return jax.shard_map(
        per_device,
        mesh=fine,
        in_specs=placed,
        out_specs=(P(SITE, None, None, None), P(SITE, TERM, None, None, None)),
        check_vma=False,
    )
```

```python
import jax
import jax.numpy as jnp
from jax import lax
from jax.experimental import pallas as pl
from jax.experimental.pallas import tpu as pltpu
from jax.sharding import Mesh, PartitionSpec as P

ITERS = 4
norm_eps = 1e-06
step_size = 0.5
SITE = ("y2", "y1", "y0", "x1", "x0", "c")
SCAN = ("c", "x0", "x1", "y0", "y1", "y2")
TERM = "z"
VMEM_LIMIT = 24 * 1024 * 1024


def halves(x):
    high = x.astype(jnp.bfloat16)
    low = (x - high.astype(jnp.float32)).astype(jnp.bfloat16)
    return high, low


def mm(a, b):
    return jnp.dot(a, b, preferred_element_type=jnp.float32)


def left_operand(a):
    return jnp.concatenate(halves(a), axis=1)


def right_operand(b):
    high, low = halves(b)
    top = jnp.concatenate([high, low], axis=1)
    return jnp.concatenate([top, top], axis=0)


def joined(a, b):
    both = mm(a, right_operand(b))
    size = b.shape[1]
    return both[:, :size] + both[:, size:]


def total(x):
    return jnp.sum(jnp.sum(x, axis=0, keepdims=True), axis=1, keepdims=True)


def krylov_kernel(z_ref, kept_ref, blocks_ref, prefix_ref, start_ref, basis_ref, moved_ref, sent_ref, left_ref, right_ref):
    groups, per_group, size, _ = blocks_ref.shape
    own = per_group // 2
    terms = groups * own
    prefix = prefix_ref[...]
    forward = left_operand(prefix)
    backward = left_operand(prefix.T)
    square = left_operand(joined(forward, prefix.T))
    squares = jnp.zeros((size, size), jnp.float32)
    for sector in range(start_ref.shape[0]):
        squares = squares + start_ref[sector] * start_ref[sector]
    x = start_ref[z_ref[0]] / jnp.sqrt(total(squares) + norm_eps)
    w = joined(forward, x)
    for group in range(groups):
        for term in range(own):
            at = (group * own + term) * size
            left_ref[at:at + size, :] = left_operand(blocks_ref[group, term])
            high, low = halves(blocks_ref[group, own + term])
            right_ref[at:at + size, :] = jnp.concatenate([high, low], axis=1)
    basis_ref[0] = x
    moved_ref[0] = w
    images = []
    growth = [jnp.ones((1, 1), jnp.float32)]
    for step in range(ITERS):
        middle = joined(left_ref[...], w)
        high, low = halves(middle)
        wide = jnp.concatenate(
            [
                jnp.concatenate([part[t * size:(t + 1) * size] for t in range(terms)], axis=1)
                for part in (high, low)
            ],
            axis=0,
        )
        both = mm(wide, right_ref[...])
        y = (both[:size, :size] + both[size:, size:]) + (both[:size, size:] + both[size:, :size])
        length = jnp.sqrt(total(y * y))
        shrink = jnp.where(length > 0.0, 1.0 / length, 0.0)
        w = joined(square, y) * shrink
        moved_ref[step + 1] = w
        images.append(y * shrink)
        growth.append(growth[step] * length)
    later = joined(backward, jnp.concatenate(images, axis=1))
    basis = [x] + [later[:, step * size:(step + 1) * size] for step in range(ITERS)]
    for step in range(ITERS):
        basis_ref[step + 1] = basis[step + 1]
    blank = jnp.zeros((1, size), jnp.float32)
    across = {}
    for i in range(ITERS + 1):
        for j in range(i, ITERS + 1):
            across[i, j] = across[j, i] = jnp.sum(basis[i] * basis[j], axis=0, keepdims=True)
    across = jnp.concatenate([across.get((i, j), blank) for i in range(8) for j in range(8)], axis=0)
    columns = lax.broadcasted_iota(jnp.int32, (64, size), 1)
    place = lax.broadcasted_iota(jnp.int32, (64, size), 0)
    held = columns < kept_ref[0, z_ref[0]]
    full = jnp.sum(across, axis=1, keepdims=True)
    held = jnp.sum(jnp.where(held, across, 0.0), axis=1, keepdims=True)
    placed = jnp.where(columns == place, full, 0.0) + jnp.where(columns == place + 64, held, 0.0)
    products = jnp.sum(placed, axis=0, keepdims=True)
    lane = lax.broadcasted_iota(jnp.int32, (1, size), 1)
    first, second = jnp.bitwise_and(lane, 56), jnp.bitwise_and(lane, 7)
    grown_first, grown_second = blank, blank
    for j in range(ITERS + 1):
        grown_first = grown_first + jnp.where(first == 8 * j, growth[j], 0.0)
        grown_second = grown_second + jnp.where(second == j, growth[j], 0.0)
    sheet = jnp.concatenate([products, grown_first, grown_second] + [blank] * 5, axis=0)
    for target in range(groups):
        sent_ref[target] = sheet


def combine_kernel(z_ref, kept_ref, scalars_ref, basis_ref, images_ref, moved_ref, sent_ref):
    sectors, _, size = scalars_ref.shape
    tiny = 1e-30

    def over(x):
        return jnp.sum(x, axis=0, keepdims=True)

    def whole(x):
        return jnp.sum(x, axis=1, keepdims=True)

    def earlier(x, count):
        return pltpu.roll(x, size - count, 1)

    def later(x, count):
        return pltpu.roll(x, count, 1)

    grown_first, grown_second = scalars_ref[:, 1, :], scalars_ref[:, 2, :]
    most_first = jnp.maximum(jnp.max(grown_first, axis=0, keepdims=True), tiny)
    most_second = jnp.maximum(jnp.max(grown_second, axis=0, keepdims=True), tiny)
    rate_first = grown_first / most_first
    rate_second = grown_second / most_second
    products = over(scalars_ref[:, 0, :] * rate_first * rate_second)
    lane = lax.broadcasted_iota(jnp.int32, (1, size), 1)
    first, second = jnp.bitwise_and(lane, 56), jnp.bitwise_and(lane, 7)
    ratio_first = jnp.where(first < 8 * ITERS, earlier(most_first, 8) / most_first, 0.0)
    ratio_second = jnp.where(second < ITERS, earlier(most_second, 1) / most_second, 0.0)
    gram = jnp.where(lane < 64, products, 0.0)
    held = jnp.where(lane < 64, 0.0, products)
    on_energy = ratio_second * earlier(gram, 1)
    on_scale = ratio_first * ratio_second * earlier(gram, 9)
    vector_first = jnp.where(first == 0, 1.0, 0.0)
    vector_second = jnp.where(second == 0, 1.0, 0.0)
    square = whole(gram * vector_first * vector_second)
    for step in range(ITERS):
        weights = vector_first * vector_second
        energy = whole(weights * on_energy)
        image_square = whole(weights * on_scale)
        rate = step_size / jnp.sqrt(image_square + norm_eps)
        keep = 1.0 + rate * energy
        update_square = keep * (keep * square - 2.0 * rate * energy) + rate * rate * image_square
        shrink = 1.0 / jnp.sqrt(update_square + norm_eps)
        keep, rate = keep * shrink, rate * shrink
        square = update_square * (shrink * shrink)
        vector_first = keep * vector_first - rate * later(ratio_first * vector_first, 8)
        vector_second = keep * vector_second - rate * later(ratio_second * vector_second, 1)
    masked = whole(held * vector_first * vector_second)
    shrink = 1.0 / jnp.sqrt(jnp.maximum(masked, 0.0) + norm_eps)
    mine = lax.broadcasted_iota(jnp.int32, (sectors, size), 0) == z_ref[0]
    factors = over(jnp.where(mine, rate_first, 0.0)) * vector_first * shrink
    result = jnp.zeros((size, size), jnp.float32)
    moved = jnp.zeros((size, size), jnp.float32)
    for j in range(ITERS + 1):
        factor = factors[:, 8 * j:8 * j + 1]
        result = result + factor * basis_ref[j]
        moved = moved + factor * images_ref[j]
    columns = lax.broadcasted_iota(jnp.int32, (size, size), 1)
    held = columns < kept_ref[0, z_ref[0]]
    result = jnp.where(held, result, 0.0)
    moved = jnp.where(held, moved, 0.0)
    moved_ref[...] = moved
    for target in range(sectors):
        sent_ref[target, 0] = result


def fill_kernel(moved_ref, _, sent_ref):
    for target in range(sent_ref.shape[0]):
        sent_ref[target, 1] = moved_ref[...]


def boundary_kernel(shared_ref, left_ref, psi_ref, out_ref):
    own, sectors, size, _ = left_ref.shape
    for sector in range(sectors):
        psi_ref[0, sector] = shared_ref[sector, 0]
        u = shared_ref[sector, 1]
        right = right_operand(u)
        across = left_operand(u.T)
        for term in range(own):
            half = mm(left_operand(left_ref[term, sector]), right)
            half = half[:, :size] + half[:, size:]
            out_ref[0, term, sector] = joined(across, half)


def vmem():
    return pl.BlockSpec(memory_space=pltpu.VMEM)


def smem():
    return pl.BlockSpec(memory_space=pltpu.SMEM)


def call(kernel, out_shape, in_specs, flops, scratch=(), aliases={}):
    return pl.pallas_call(
        kernel,
        out_shape=out_shape,
        in_specs=in_specs,
        out_specs=jax.tree.map(lambda _: vmem(), out_shape),
        scratch_shapes=scratch,
        input_output_aliases=aliases,
        compiler_params=pltpu.CompilerParams(vmem_limit_bytes=VMEM_LIMIT),
        cost_estimate=pl.CostEstimate(flops=flops, bytes_accessed=4 << 20, transcendentals=0),
    )


def struct(*shape):
    return jax.ShapeDtypeStruct(shape, jnp.float32)


def product(a, b):
    return jnp.dot(a, b, precision=lax.Precision.HIGHEST, preferred_element_type=jnp.float32)


def scanned(own):
    whole = own
    prefix = None
    middle = None
    for level, axis in enumerate(SCAN):
        with jax.named_scope("scan_" + axis):
            pair = lax.all_gather(whole, axis)
            upper = lax.axis_index(axis) == 1
            if prefix is None:
                prefix = jnp.where(upper, pair[0], jnp.eye(own.shape[0], dtype=own.dtype))
            else:
                prefix = jnp.where(upper, product(pair[0], prefix), prefix)
            if level + 1 < len(SCAN):
                whole = product(pair[0], pair[1])
            if axis == "x1":
                middle = whole
    return prefix, middle


def per_device(left_env, right_env, transfer, psi_start, kept):
    left, right, transfer, psi = left_env[0], right_env[0], transfer[0], psi_start[0]
    own, sectors, size, _ = left.shape
    z = lax.axis_index(TERM)
    spot = z[None]
    pairs = [(source, source + 1) for source in range(63)]
    with jax.named_scope("gather_terms"):
        outgoing = jnp.concatenate([left, right], axis=0)
        blocks = lax.all_to_all(outgoing, TERM, 1, 0, tiled=False)
    with jax.named_scope("prefix"):
        prefix, middle = scanned(lax.dynamic_index_in_dim(transfer, z, 0, keepdims=False))
    with jax.named_scope("left_previous"):
        late, _ = lax.optimization_barrier((left, middle))
        left_previous = lax.ppermute(late, SITE, pairs)
    with jax.named_scope("krylov"):
        terms = own * sectors
        prefix, left_previous = lax.optimization_barrier((prefix, left_previous))
        basis, images, sent = call(
            krylov_kernel,
            (struct(ITERS + 1, size, size), struct(ITERS + 1, size, size), struct(sectors, 8, size)),
            [smem(), smem(), vmem(), vmem(), vmem()],
            ITERS * terms * 4 * 2 * 3 * size**3,
            [pltpu.VMEM((terms * size, 2 * size), jnp.bfloat16)] * 2,
        )(spot, kept, blocks, prefix, psi)
    with jax.named_scope("share_scalars"):
        scalars = lax.all_to_all(sent, TERM, 0, 0, tiled=True)
    with jax.named_scope("combine"):
        moved, sent = call(
            combine_kernel,
            (struct(size, size), struct(sectors, 2, size, size)),
            [smem(), smem()] + [vmem()] * 3,
            size**2 * 100,
        )(spot, kept, scalars, basis, images)
    with jax.named_scope("hand_on"):
        moved = lax.ppermute(moved, SITE, pairs)
    with jax.named_scope("share"):
        sent = call(
            fill_kernel,
            struct(sectors, 2, size, size),
            [vmem(), vmem()],
            size**2,
            aliases={1: 0},
        )(moved, sent)
        shared = lax.all_to_all(sent, TERM, 0, 0, tiled=True)
    with jax.named_scope("boundary"):
        result, incoming = call(
            boundary_kernel,
            (struct(1, sectors, size, size), struct(1, own, sectors, size, size)),
            [vmem(), vmem()],
            own * sectors * 12 * size**3,
        )(shared, left_previous)
    return result, incoming


def solution(mesh):
    fine = Mesh(mesh.devices.reshape((2,) * 6 + (8,)), SITE + (TERM,))
    placed = (
        P(SITE, TERM, None, None, None),
        P(SITE, TERM, None, None, None),
        P(SITE, None, None, None),
        P(SITE, None, None, None),
        P(SITE, None),
    )
    return jax.shard_map(
        per_device,
        mesh=fine,
        in_specs=placed,
        out_specs=(P(SITE, None, None, None), P(SITE, TERM, None, None, None)),
        check_vma=False,
    )
```

```python
import jax
import jax.numpy as jnp
from jax import lax
from jax.experimental import pallas as pl
from jax.experimental.pallas import tpu as pltpu
from jax.sharding import Mesh, PartitionSpec as P

ITERS = 4
norm_eps = 1e-06
step_size = 0.5
SITE = ("y2", "y1", "y0", "x1", "x0", "c")
SCAN = ("c", "x0", "x1", "y0", "y1", "y2")
TERM = "z"
FIRST = (0, 4, 2, 6, 1, 5, 3, 7)
OWNERS = sum(place << (4 * at) for place, at in enumerate(FIRST))
LAST = (7, 6, 5, 4, 3, 2, 1, 0)
VMEM_LIMIT = 24 * 1024 * 1024


def halves(x):
    high = x.astype(jnp.bfloat16)
    low = (x - high.astype(jnp.float32)).astype(jnp.bfloat16)
    return high, low


def mm(a, b):
    return jnp.dot(a, b, preferred_element_type=jnp.float32)


def left_operand(a):
    return jnp.concatenate(halves(a), axis=1)


def right_operand(b):
    high, low = halves(b)
    top = jnp.concatenate([high, low], axis=1)
    return jnp.concatenate([top, top], axis=0)


def joined(a, b):
    both = mm(a, right_operand(b))
    size = b.shape[1]
    return both[:, :size] + both[:, size:]


def total(x):
    return jnp.sum(jnp.sum(x, axis=0, keepdims=True), axis=1, keepdims=True)


def krylov_kernel(z_ref, kept_ref, blocks_ref, prefix_ref, start_ref, basis_ref, moved_ref, sent_ref, left_ref, right_ref):
    groups, per_group, size, _ = blocks_ref.shape
    own = per_group // 2
    terms = groups * own
    prefix = prefix_ref[...]
    forward = left_operand(prefix)
    backward = left_operand(prefix.T)
    square = left_operand(joined(forward, prefix.T))
    squares = jnp.zeros((size, size), jnp.float32)
    for sector in range(start_ref.shape[0]):
        squares = squares + start_ref[sector] * start_ref[sector]
    x = start_ref[z_ref[0]] / jnp.sqrt(total(squares) + norm_eps)
    w = joined(forward, x)
    for group in range(groups):
        for term in range(own):
            at = (group * own + term) * size
            left_ref[at:at + size, :] = left_operand(blocks_ref[group, term])
            high, low = halves(blocks_ref[group, own + term])
            right_ref[at:at + size, :] = jnp.concatenate([high, low], axis=1)
    basis_ref[0] = x
    moved_ref[0] = w
    images = []
    growth = [jnp.ones((1, 1), jnp.float32)]
    for step in range(ITERS):
        middle = joined(left_ref[...], w)
        high, low = halves(middle)
        wide = jnp.concatenate(
            [
                jnp.concatenate([part[t * size:(t + 1) * size] for t in range(terms)], axis=1)
                for part in (high, low)
            ],
            axis=0,
        )
        both = mm(wide, right_ref[...])
        y = (both[:size, :size] + both[size:, size:]) + (both[:size, size:] + both[size:, :size])
        length = jnp.sqrt(total(y * y))
        shrink = jnp.where(length > 0.0, 1.0 / length, 0.0)
        w = joined(square, y) * shrink
        moved_ref[step + 1] = w
        images.append(y * shrink)
        growth.append(growth[step] * length)
    later = joined(backward, jnp.concatenate(images, axis=1))
    basis = [x] + [later[:, step * size:(step + 1) * size] for step in range(ITERS)]
    for step in range(ITERS):
        basis_ref[step + 1] = basis[step + 1]
    blank = jnp.zeros((1, size), jnp.float32)
    across = {}
    for i in range(ITERS + 1):
        for j in range(i, ITERS + 1):
            across[i, j] = across[j, i] = jnp.sum(basis[i] * basis[j], axis=0, keepdims=True)
    across = jnp.concatenate([across.get((i, j), blank) for i in range(8) for j in range(8)], axis=0)
    columns = lax.broadcasted_iota(jnp.int32, (64, size), 1)
    place = lax.broadcasted_iota(jnp.int32, (64, size), 0)
    held = columns < kept_ref[0, z_ref[0]]
    full = jnp.sum(across, axis=1, keepdims=True)
    held = jnp.sum(jnp.where(held, across, 0.0), axis=1, keepdims=True)
    placed = jnp.where(columns == place, full, 0.0) + jnp.where(columns == place + 64, held, 0.0)
    products = jnp.sum(placed, axis=0, keepdims=True)
    lane = lax.broadcasted_iota(jnp.int32, (1, size), 1)
    first, second = jnp.bitwise_and(lane, 56), jnp.bitwise_and(lane, 7)
    grown_first, grown_second = blank, blank
    for j in range(ITERS + 1):
        grown_first = grown_first + jnp.where(first == 8 * j, growth[j], 0.0)
        grown_second = grown_second + jnp.where(second == j, growth[j], 0.0)
    sheet = jnp.concatenate([products, grown_first, grown_second] + [blank] * 5, axis=0)
    for target in range(groups):
        sent_ref[target] = sheet


def combine_kernel(z_ref, kept_ref, scalars_ref, basis_ref, images_ref, moved_ref, sent_ref):
    sectors, _, size = scalars_ref.shape
    tiny = 1e-30

    def over(x):
        return jnp.sum(x, axis=0, keepdims=True)

    def whole(x):
        return jnp.sum(x, axis=1, keepdims=True)

    def earlier(x, count):
        return pltpu.roll(x, size - count, 1)

    def later(x, count):
        return pltpu.roll(x, count, 1)

    grown_first, grown_second = scalars_ref[:, 1, :], scalars_ref[:, 2, :]
    most_first = jnp.maximum(jnp.max(grown_first, axis=0, keepdims=True), tiny)
    most_second = jnp.maximum(jnp.max(grown_second, axis=0, keepdims=True), tiny)
    rate_first = grown_first / most_first
    rate_second = grown_second / most_second
    products = over(scalars_ref[:, 0, :] * rate_first * rate_second)
    lane = lax.broadcasted_iota(jnp.int32, (1, size), 1)
    first, second = jnp.bitwise_and(lane, 56), jnp.bitwise_and(lane, 7)
    ratio_first = jnp.where(first < 8 * ITERS, earlier(most_first, 8) / most_first, 0.0)
    ratio_second = jnp.where(second < ITERS, earlier(most_second, 1) / most_second, 0.0)
    gram = jnp.where(lane < 64, products, 0.0)
    held = jnp.where(lane < 64, 0.0, products)
    on_energy = ratio_second * earlier(gram, 1)
    on_scale = ratio_first * ratio_second * earlier(gram, 9)
    vector_first = jnp.where(first == 0, 1.0, 0.0)
    vector_second = jnp.where(second == 0, 1.0, 0.0)
    square = whole(gram * vector_first * vector_second)
    for step in range(ITERS):
        weights = vector_first * vector_second
        energy = whole(weights * on_energy)
        image_square = whole(weights * on_scale)
        rate = step_size / jnp.sqrt(image_square + norm_eps)
        keep = 1.0 + rate * energy
        update_square = keep * (keep * square - 2.0 * rate * energy) + rate * rate * image_square
        shrink = 1.0 / jnp.sqrt(update_square + norm_eps)
        keep, rate = keep * shrink, rate * shrink
        square = update_square * (shrink * shrink)
        vector_first = keep * vector_first - rate * later(ratio_first * vector_first, 8)
        vector_second = keep * vector_second - rate * later(ratio_second * vector_second, 1)
    masked = whole(held * vector_first * vector_second)
    shrink = 1.0 / jnp.sqrt(jnp.maximum(masked, 0.0) + norm_eps)
    mine = lax.broadcasted_iota(jnp.int32, (sectors, size), 0) == z_ref[0]
    factors = over(jnp.where(mine, rate_first, 0.0)) * vector_first * shrink
    result = jnp.zeros((size, size), jnp.float32)
    moved = jnp.zeros((size, size), jnp.float32)
    for j in range(ITERS + 1):
        factor = factors[:, 8 * j:8 * j + 1]
        result = result + factor * basis_ref[j]
        moved = moved + factor * images_ref[j]
    columns = lax.broadcasted_iota(jnp.int32, (size, size), 1)
    held = columns < kept_ref[0, z_ref[0]]
    result = jnp.where(held, result, 0.0)
    moved = jnp.where(held, moved, 0.0)
    moved_ref[...] = moved
    for target in range(sectors):
        sent_ref[target, 0] = result


def fill_kernel(moved_ref, _, sent_ref):
    for target in range(sent_ref.shape[0]):
        sent_ref[target, 1] = moved_ref[...]


def boundary_kernel(shared_ref, left_ref, psi_ref, out_ref, made_ref, sems):
    own, sectors, size, _ = left_ref.shape
    copies = []
    for sector in range(sectors):
        at = LAST.index(FIRST[sector])
        copies.append(pltpu.make_async_copy(shared_ref.at[at, 0], psi_ref.at[0, sector], sems.at[sector]))
        copies[-1].start()
    for sector in range(sectors):
        u = shared_ref[LAST.index(FIRST[sector]), 1]
        right = right_operand(u)
        across = left_operand(u.T)
        for term in range(own):
            half = mm(left_operand(left_ref[term, sector]), right)
            half = half[:, :size] + half[:, size:]
            made_ref[sector, term] = joined(across, half)
        copies.append(pltpu.make_async_copy(made_ref.at[sector], out_ref.at[0, :, sector], sems.at[sectors + sector]))
        copies[-1].start()
    for copy in copies:
        copy.wait()


def vmem():
    return pl.BlockSpec(memory_space=pltpu.VMEM)


def smem():
    return pl.BlockSpec(memory_space=pltpu.SMEM)


def call(kernel, out_shape, in_specs, flops, scratch=(), aliases={}, out_spec=pl.BlockSpec(memory_space=pltpu.VMEM)):
    return pl.pallas_call(
        kernel,
        out_shape=out_shape,
        in_specs=in_specs,
        out_specs=jax.tree.map(lambda _: out_spec, out_shape),
        scratch_shapes=scratch,
        input_output_aliases=aliases,
        compiler_params=pltpu.CompilerParams(vmem_limit_bytes=VMEM_LIMIT),
        cost_estimate=pl.CostEstimate(flops=flops, bytes_accessed=4 << 20, transcendentals=0),
    )


def struct(*shape):
    return jax.ShapeDtypeStruct(shape, jnp.float32)


def product(a, b):
    return jnp.dot(a, b, precision=lax.Precision.HIGHEST, preferred_element_type=jnp.float32)


def scanned(own):
    whole = own
    prefix = None
    for level, axis in enumerate(SCAN):
        with jax.named_scope("scan_" + axis):
            pair = lax.all_gather(whole, axis)
            upper = lax.axis_index(axis) == 1
            if prefix is None:
                prefix = jnp.where(upper, pair[0], jnp.eye(own.shape[0], dtype=own.dtype))
            else:
                prefix = jnp.where(upper, product(pair[0], prefix), prefix)
            if level + 1 < len(SCAN):
                whole = product(pair[0], pair[1])
    return prefix


def per_device(left_env, right_env, transfer, psi_start, kept):
    left, right, transfer, psi = left_env[0], right_env[0], transfer[0], psi_start[0]
    own, sectors, size, _ = left.shape
    z = lax.axis_index(TERM)
    z = jnp.bitwise_and(jnp.right_shift(jnp.int32(OWNERS), 4 * z), 7)
    spot = z[None]
    pairs = [(source, source + 1) for source in range(63)]
    with jax.named_scope("gather_terms"):
        outgoing = jnp.concatenate([left, right], axis=0)
        blocks = lax.all_to_all(outgoing, TERM, 1, 0, axis_index_groups=[list(FIRST)], tiled=False)
    with jax.named_scope("prefix"):
        prefix = scanned(lax.dynamic_index_in_dim(transfer, z, 0, keepdims=False))
    with jax.named_scope("left_previous"):
        late, _ = lax.optimization_barrier((left, prefix))
        left_previous = lax.ppermute(late, SITE, pairs)
    with jax.named_scope("krylov"):
        terms = own * sectors
        basis, images, sent = call(
            krylov_kernel,
            (struct(ITERS + 1, size, size), struct(ITERS + 1, size, size), struct(sectors, 8, size)),
            [smem(), smem(), vmem(), vmem(), vmem()],
            ITERS * terms * 4 * 2 * 3 * size**3,
            [pltpu.VMEM((terms * size, 2 * size), jnp.bfloat16)] * 2,
        )(spot, kept, blocks, prefix, psi)
    with jax.named_scope("share_scalars"):
        scalars = lax.all_to_all(sent, TERM, 0, 0, axis_index_groups=[list(FIRST)], tiled=True)
    with jax.named_scope("combine"):
        moved, sent = call(
            combine_kernel,
            (struct(size, size), struct(sectors, 2, size, size)),
            [smem(), smem()] + [vmem()] * 3,
            size**2 * 100,
        )(spot, kept, scalars, basis, images)
    with jax.named_scope("hand_on"):
        moved, left_previous = lax.optimization_barrier((moved, left_previous))
        moved = lax.ppermute(moved, SITE, pairs)
    with jax.named_scope("share"):
        sent = call(
            fill_kernel,
            struct(sectors, 2, size, size),
            [vmem(), vmem()],
            size**2,
            aliases={1: 0},
        )(moved, sent)
        shared = lax.all_to_all(sent, TERM, 0, 0, axis_index_groups=[list(LAST)], tiled=True)
    with jax.named_scope("boundary"):
        result, incoming = call(
            boundary_kernel,
            (struct(1, sectors, size, size), struct(1, own, sectors, size, size)),
            [vmem(), vmem()],
            own * sectors * 12 * size**3,
            [pltpu.VMEM((sectors, own, size, size), jnp.float32), pltpu.SemaphoreType.DMA((2 * sectors,))],
            out_spec=pl.BlockSpec(memory_space=pl.ANY),
        )(shared, left_previous)
    return result, incoming


def solution(mesh):
    fine = Mesh(mesh.devices.reshape((2,) * 6 + (8,)), SITE + (TERM,))
    placed = (
        P(SITE, TERM, None, None, None),
        P(SITE, TERM, None, None, None),
        P(SITE, None, None, None),
        P(SITE, None, None, None),
        P(SITE, None),
    )
    return jax.shard_map(
        per_device,
        mesh=fine,
        in_specs=placed,
        out_specs=(P(SITE, None, None, None), P(SITE, TERM, None, None, None)),
        check_vma=False,
    )
```

```python
import jax
import jax.numpy as jnp
from jax import lax
from jax.experimental import pallas as pl
from jax.experimental.pallas import tpu as pltpu
from jax.sharding import Mesh, PartitionSpec as P

ITERS = 4
norm_eps = 1e-06
step_size = 0.5
SITE = ("y2", "y1", "y0", "x1", "x0", "c")
SCAN = ("c", "x0", "x1", "y0", "y1", "y2")
TERM = "z"
FIRST = (0, 4, 2, 6, 1, 5, 3, 7)
OWNERS = sum(place << (4 * at) for place, at in enumerate(FIRST))
LAST = (7, 6, 5, 4, 3, 2, 1, 0)
VMEM_LIMIT = 24 * 1024 * 1024


def halves(x):
    high = x.astype(jnp.bfloat16)
    low = (x - high.astype(jnp.float32)).astype(jnp.bfloat16)
    return high, low


def mm(a, b):
    return jnp.dot(a, b, preferred_element_type=jnp.float32)


def left_operand(a):
    return jnp.concatenate(halves(a), axis=1)


def right_operand(b):
    high, low = halves(b)
    top = jnp.concatenate([high, low], axis=1)
    return jnp.concatenate([top, top], axis=0)


def joined(a, b):
    both = mm(a, right_operand(b))
    size = b.shape[1]
    return both[:, :size] + both[:, size:]


def total(x):
    return jnp.sum(jnp.sum(x, axis=0, keepdims=True), axis=1, keepdims=True)


def krylov_kernel(z_ref, kept_ref, blocks_ref, prefix_ref, start_ref, basis_ref, moved_ref, sent_ref, left_ref, right_ref):
    groups, per_group, size, _ = blocks_ref.shape
    own = per_group // 2
    terms = groups * own
    prefix = prefix_ref[...]
    forward = left_operand(prefix)
    backward = left_operand(prefix.T)
    square = left_operand(joined(forward, prefix.T))
    squares = jnp.zeros((size, size), jnp.float32)
    for sector in range(start_ref.shape[0]):
        squares = squares + start_ref[sector] * start_ref[sector]
    x = start_ref[z_ref[0]] / jnp.sqrt(total(squares) + norm_eps)
    w = joined(forward, x)
    for group in range(groups):
        for term in range(own):
            at = (group * own + term) * size
            left_ref[at:at + size, :] = left_operand(blocks_ref[group, term])
            high, low = halves(blocks_ref[group, own + term])
            right_ref[at:at + size, :] = jnp.concatenate([high, low], axis=1)
    basis_ref[0] = x
    moved_ref[0] = w
    images = []
    growth = [jnp.ones((1, 1), jnp.float32)]
    for step in range(ITERS):
        middle = joined(left_ref[...], w)
        high, low = halves(middle)
        wide = jnp.concatenate(
            [
                jnp.concatenate([part[t * size:(t + 1) * size] for t in range(terms)], axis=1)
                for part in (high, low)
            ],
            axis=0,
        )
        both = mm(wide, right_ref[...])
        y = (both[:size, :size] + both[size:, size:]) + (both[:size, size:] + both[size:, :size])
        length = jnp.sqrt(total(y * y))
        shrink = jnp.where(length > 0.0, 1.0 / length, 0.0)
        w = joined(square, y) * shrink
        moved_ref[step + 1] = w
        images.append(y * shrink)
        growth.append(growth[step] * length)
    later = joined(backward, jnp.concatenate(images, axis=1))
    basis = [x] + [later[:, step * size:(step + 1) * size] for step in range(ITERS)]
    for step in range(ITERS):
        basis_ref[step + 1] = basis[step + 1]
    blank = jnp.zeros((1, size), jnp.float32)
    across = {}
    for i in range(ITERS + 1):
        for j in range(i, ITERS + 1):
            across[i, j] = across[j, i] = jnp.sum(basis[i] * basis[j], axis=0, keepdims=True)
    across = jnp.concatenate([across.get((i, j), blank) for i in range(8) for j in range(8)], axis=0)
    columns = lax.broadcasted_iota(jnp.int32, (64, size), 1)
    place = lax.broadcasted_iota(jnp.int32, (64, size), 0)
    held = columns < kept_ref[0, z_ref[0]]
    full = jnp.sum(across, axis=1, keepdims=True)
    held = jnp.sum(jnp.where(held, across, 0.0), axis=1, keepdims=True)
    placed = jnp.where(columns == place, full, 0.0) + jnp.where(columns == place + 64, held, 0.0)
    products = jnp.sum(placed, axis=0, keepdims=True)
    lane = lax.broadcasted_iota(jnp.int32, (1, size), 1)
    first, second = jnp.bitwise_and(lane, 56), jnp.bitwise_and(lane, 7)
    grown_first, grown_second = blank, blank
    for j in range(ITERS + 1):
        grown_first = grown_first + jnp.where(first == 8 * j, growth[j], 0.0)
        grown_second = grown_second + jnp.where(second == j, growth[j], 0.0)
    sheet = jnp.concatenate([products, grown_first, grown_second] + [blank] * 5, axis=0)
    for target in range(groups):
        sent_ref[target] = sheet


def combine_kernel(z_ref, kept_ref, scalars_ref, basis_ref, images_ref, moved_ref, sent_ref):
    sectors, _, size = scalars_ref.shape
    tiny = 1e-30

    def over(x):
        return jnp.sum(x, axis=0, keepdims=True)

    def whole(x):
        return jnp.sum(x, axis=1, keepdims=True)

    def earlier(x, count):
        return pltpu.roll(x, size - count, 1)

    def later(x, count):
        return pltpu.roll(x, count, 1)

    grown_first, grown_second = scalars_ref[:, 1, :], scalars_ref[:, 2, :]
    most_first = jnp.maximum(jnp.max(grown_first, axis=0, keepdims=True), tiny)
    most_second = jnp.maximum(jnp.max(grown_second, axis=0, keepdims=True), tiny)
    rate_first = grown_first / most_first
    rate_second = grown_second / most_second
    products = over(scalars_ref[:, 0, :] * rate_first * rate_second)
    lane = lax.broadcasted_iota(jnp.int32, (1, size), 1)
    first, second = jnp.bitwise_and(lane, 56), jnp.bitwise_and(lane, 7)
    ratio_first = jnp.where(first < 8 * ITERS, earlier(most_first, 8) / most_first, 0.0)
    ratio_second = jnp.where(second < ITERS, earlier(most_second, 1) / most_second, 0.0)
    gram = jnp.where(lane < 64, products, 0.0)
    held = jnp.where(lane < 64, 0.0, products)
    on_energy = ratio_second * earlier(gram, 1)
    on_scale = ratio_first * ratio_second * earlier(gram, 9)
    vector_first = jnp.where(first == 0, 1.0, 0.0)
    vector_second = jnp.where(second == 0, 1.0, 0.0)
    square = whole(gram * vector_first * vector_second)
    for step in range(ITERS):
        weights = vector_first * vector_second
        energy = whole(weights * on_energy)
        image_square = whole(weights * on_scale)
        rate = step_size / jnp.sqrt(image_square + norm_eps)
        keep = 1.0 + rate * energy
        update_square = keep * (keep * square - 2.0 * rate * energy) + rate * rate * image_square
        shrink = 1.0 / jnp.sqrt(update_square + norm_eps)
        keep, rate = keep * shrink, rate * shrink
        square = update_square * (shrink * shrink)
        vector_first = keep * vector_first - rate * later(ratio_first * vector_first, 8)
        vector_second = keep * vector_second - rate * later(ratio_second * vector_second, 1)
    masked = whole(held * vector_first * vector_second)
    shrink = 1.0 / jnp.sqrt(jnp.maximum(masked, 0.0) + norm_eps)
    mine = lax.broadcasted_iota(jnp.int32, (sectors, size), 0) == z_ref[0]
    factors = over(jnp.where(mine, rate_first, 0.0)) * vector_first * shrink
    result = jnp.zeros((size, size), jnp.float32)
    moved = jnp.zeros((size, size), jnp.float32)
    for j in range(ITERS + 1):
        factor = factors[:, 8 * j:8 * j + 1]
        result = result + factor * basis_ref[j]
        moved = moved + factor * images_ref[j]
    columns = lax.broadcasted_iota(jnp.int32, (size, size), 1)
    held = columns < kept_ref[0, z_ref[0]]
    result = jnp.where(held, result, 0.0)
    moved = jnp.where(held, moved, 0.0)
    moved_ref[...] = moved
    for target in range(sectors):
        sent_ref[target, 0] = result


def fill_kernel(moved_ref, _, sent_ref):
    for target in range(sent_ref.shape[0]):
        sent_ref[target, 1] = moved_ref[...]


def stage_kernel(left_ref, out_ref):
    own, sectors, _, _ = left_ref.shape
    for term in range(own):
        for sector in range(sectors):
            out_ref[term, sector] = left_operand(left_ref[term, sector])


def boundary_kernel(shared_ref, left_ref, psi_ref, out_ref, made_ref, sems):
    own, sectors, size, _ = left_ref.shape
    copies = []
    for sector in range(sectors):
        at = LAST.index(FIRST[sector])
        copies.append(pltpu.make_async_copy(shared_ref.at[at, 0], psi_ref.at[0, sector], sems.at[sector]))
        copies[-1].start()
    for sector in range(sectors):
        u = shared_ref[LAST.index(FIRST[sector]), 1]
        right = right_operand(u)
        across = left_operand(u.T)
        for term in range(own):
            half = mm(left_ref[term, sector], right)
            half = half[:, :size] + half[:, size:]
            made_ref[sector, term] = joined(across, half)
        copies.append(pltpu.make_async_copy(made_ref.at[sector], out_ref.at[0, :, sector], sems.at[sectors + sector]))
        copies[-1].start()
    for copy in copies:
        copy.wait()


def vmem():
    return pl.BlockSpec(memory_space=pltpu.VMEM)


def smem():
    return pl.BlockSpec(memory_space=pltpu.SMEM)


def call(kernel, out_shape, in_specs, flops, scratch=(), aliases={}, out_spec=pl.BlockSpec(memory_space=pltpu.VMEM)):
    return pl.pallas_call(
        kernel,
        out_shape=out_shape,
        in_specs=in_specs,
        out_specs=jax.tree.map(lambda _: out_spec, out_shape),
        scratch_shapes=scratch,
        input_output_aliases=aliases,
        compiler_params=pltpu.CompilerParams(vmem_limit_bytes=VMEM_LIMIT),
        cost_estimate=pl.CostEstimate(flops=flops, bytes_accessed=4 << 20, transcendentals=0),
    )


def struct(*shape):
    return jax.ShapeDtypeStruct(shape, jnp.float32)


def product(a, b):
    return jnp.dot(a, b, precision=lax.Precision.HIGHEST, preferred_element_type=jnp.float32)


def scanned(own):
    whole = own
    prefix = None
    for level, axis in enumerate(SCAN):
        with jax.named_scope("scan_" + axis):
            pair = lax.all_gather(whole, axis)
            upper = lax.axis_index(axis) == 1
            if prefix is None:
                prefix = jnp.where(upper, pair[0], jnp.eye(own.shape[0], dtype=own.dtype))
            else:
                prefix = jnp.where(upper, product(pair[0], prefix), prefix)
            if level + 1 < len(SCAN):
                whole = product(pair[0], pair[1])
    return prefix


def per_device(left_env, right_env, transfer, psi_start, kept):
    left, right, transfer, psi = left_env[0], right_env[0], transfer[0], psi_start[0]
    own, sectors, size, _ = left.shape
    z = lax.axis_index(TERM)
    z = jnp.bitwise_and(jnp.right_shift(jnp.int32(OWNERS), 4 * z), 7)
    spot = z[None]
    pairs = [(source, source + 1) for source in range(63)]
    with jax.named_scope("gather_terms"):
        outgoing = jnp.concatenate([left, right], axis=0)
        blocks = lax.all_to_all(outgoing, TERM, 1, 0, axis_index_groups=[list(FIRST)], tiled=False)
    with jax.named_scope("prefix"):
        prefix = scanned(lax.dynamic_index_in_dim(transfer, z, 0, keepdims=False))
    with jax.named_scope("left_previous"):
        late, _ = lax.optimization_barrier((left, prefix))
        left_previous = lax.ppermute(late, SITE, pairs)
    with jax.named_scope("krylov"):
        terms = own * sectors
        basis, images, sent = call(
            krylov_kernel,
            (struct(ITERS + 1, size, size), struct(ITERS + 1, size, size), struct(sectors, 8, size)),
            [smem(), smem(), vmem(), vmem(), vmem()],
            ITERS * terms * 4 * 2 * 3 * size**3,
            [pltpu.VMEM((terms * size, 2 * size), jnp.bfloat16)] * 2,
        )(spot, kept, blocks, prefix, psi)
    with jax.named_scope("share_scalars"):
        scalars = lax.all_to_all(sent, TERM, 0, 0, axis_index_groups=[list(FIRST)], tiled=True)
    with jax.named_scope("combine"):
        moved, sent = call(
            combine_kernel,
            (struct(size, size), struct(sectors, 2, size, size)),
            [smem(), smem()] + [vmem()] * 3,
            size**2 * 100,
        )(spot, kept, scalars, basis, images)
    with jax.named_scope("hand_on"):
        moved, left_previous = lax.optimization_barrier((moved, left_previous))
        moved = lax.ppermute(moved, SITE, pairs)
        staged = call(
            stage_kernel,
            jax.ShapeDtypeStruct((own, sectors, size, 2 * size), jnp.bfloat16),
            [vmem()],
            own * sectors * size**3,
        )(left_previous)
        moved, staged = lax.optimization_barrier((moved, staged))
    with jax.named_scope("share"):
        sent = call(
            fill_kernel,
            struct(sectors, 2, size, size),
            [vmem(), vmem()],
            size**2,
            aliases={1: 0},
        )(moved, sent)
        shared = lax.all_to_all(sent, TERM, 0, 0, axis_index_groups=[list(LAST)], tiled=True)
    with jax.named_scope("boundary"):
        result, incoming = call(
            boundary_kernel,
            (struct(1, sectors, size, size), struct(1, own, sectors, size, size)),
            [vmem(), vmem()],
            own * sectors * 12 * size**3,
            [pltpu.VMEM((sectors, own, size, size), jnp.float32), pltpu.SemaphoreType.DMA((2 * sectors,))],
            out_spec=pl.BlockSpec(memory_space=pl.ANY),
        )(shared, staged)
    return result, incoming


def solution(mesh):
    fine = Mesh(mesh.devices.reshape((2,) * 6 + (8,)), SITE + (TERM,))
    placed = (
        P(SITE, TERM, None, None, None),
        P(SITE, TERM, None, None, None),
        P(SITE, None, None, None),
        P(SITE, None, None, None),
        P(SITE, None),
    )
    return jax.shard_map(
        per_device,
        mesh=fine,
        in_specs=placed,
        out_specs=(P(SITE, None, None, None), P(SITE, TERM, None, None, None)),
        check_vma=False,
    )
```

```python
import jax
import jax.numpy as jnp
from jax import lax
from jax.experimental import pallas as pl
from jax.experimental.pallas import tpu as pltpu
from jax.sharding import Mesh, PartitionSpec as P

ITERS = 4
norm_eps = 1e-06
step_size = 0.5
SITE = ("y2", "y1", "y0", "x1", "x0", "c")
SCAN = ("c", "x0", "x1", "y0", "y1", "y2")
TERM = "z"
FIRST = (0, 4, 1, 5, 2, 6, 3, 7)
OWNERS = sum(place << (4 * at) for place, at in enumerate(FIRST))
LAST = (7, 6, 5, 4, 3, 2, 1, 0)
VMEM_LIMIT = 24 * 1024 * 1024


def halves(x):
    high = x.astype(jnp.bfloat16)
    low = (x - high.astype(jnp.float32)).astype(jnp.bfloat16)
    return high, low


def mm(a, b):
    return jnp.dot(a, b, preferred_element_type=jnp.float32)


def left_operand(a):
    return jnp.concatenate(halves(a), axis=1)


def right_operand(b):
    high, low = halves(b)
    top = jnp.concatenate([high, low], axis=1)
    return jnp.concatenate([top, top], axis=0)


def joined(a, b):
    both = mm(a, right_operand(b))
    size = b.shape[1]
    return both[:, :size] + both[:, size:]


def total(x):
    return jnp.sum(jnp.sum(x, axis=0, keepdims=True), axis=1, keepdims=True)


def prepare_kernel(z_ref, prefix_ref, start_ref, x_ref, w_ref, backward_ref, square_ref):
    sectors, size, _ = start_ref.shape
    prefix = prefix_ref[...]
    forward = left_operand(prefix)
    backward_ref[...] = left_operand(prefix.T)
    square_ref[...] = left_operand(joined(forward, prefix.T))
    squares = jnp.zeros((size, size), jnp.float32)
    for sector in range(sectors):
        squares = squares + start_ref[sector] * start_ref[sector]
    x = start_ref[z_ref[0]] / jnp.sqrt(total(squares) + norm_eps)
    x_ref[...] = x
    w_ref[...] = joined(forward, x)


def krylov_kernel(z_ref, kept_ref, blocks_ref, x_ref, w_ref, backward_ref, square_ref, basis_ref, moved_ref, sent_ref, left_ref, right_ref):
    groups, per_group, size, _ = blocks_ref.shape
    own = per_group // 2
    terms = groups * own
    x, w = x_ref[...], w_ref[...]
    backward, square = backward_ref[...], square_ref[...]
    for group in range(groups):
        for term in range(own):
            at = (group * own + term) * size
            left_ref[at:at + size, :] = left_operand(blocks_ref[group, term])
            high, low = halves(blocks_ref[group, own + term])
            right_ref[at:at + size, :] = jnp.concatenate([high, low], axis=1)
    basis_ref[0] = x
    moved_ref[0] = w
    images = []
    growth = [jnp.ones((1, 1), jnp.float32)]
    for step in range(ITERS):
        middle = joined(left_ref[...], w)
        high, low = halves(middle)
        wide = jnp.concatenate(
            [
                jnp.concatenate([part[t * size:(t + 1) * size] for t in range(terms)], axis=1)
                for part in (high, low)
            ],
            axis=0,
        )
        both = mm(wide, right_ref[...])
        y = (both[:size, :size] + both[size:, size:]) + (both[:size, size:] + both[size:, :size])
        length = jnp.sqrt(total(y * y))
        shrink = jnp.where(length > 0.0, 1.0 / length, 0.0)
        w = joined(square, y) * shrink
        moved_ref[step + 1] = w
        images.append(y * shrink)
        growth.append(growth[step] * length)
    later = joined(backward, jnp.concatenate(images, axis=1))
    basis = [x] + [later[:, step * size:(step + 1) * size] for step in range(ITERS)]
    for step in range(ITERS):
        basis_ref[step + 1] = basis[step + 1]
    blank = jnp.zeros((1, size), jnp.float32)
    across = {}
    for i in range(ITERS + 1):
        for j in range(i, ITERS + 1):
            across[i, j] = across[j, i] = jnp.sum(basis[i] * basis[j], axis=0, keepdims=True)
    across = jnp.concatenate([across.get((i, j), blank) for i in range(8) for j in range(8)], axis=0)
    columns = lax.broadcasted_iota(jnp.int32, (64, size), 1)
    place = lax.broadcasted_iota(jnp.int32, (64, size), 0)
    held = columns < kept_ref[0, z_ref[0]]
    full = jnp.sum(across, axis=1, keepdims=True)
    held = jnp.sum(jnp.where(held, across, 0.0), axis=1, keepdims=True)
    placed = jnp.where(columns == place, full, 0.0) + jnp.where(columns == place + 64, held, 0.0)
    products = jnp.sum(placed, axis=0, keepdims=True)
    lane = lax.broadcasted_iota(jnp.int32, (1, size), 1)
    first, second = jnp.bitwise_and(lane, 56), jnp.bitwise_and(lane, 7)
    grown_first, grown_second = blank, blank
    for j in range(ITERS + 1):
        grown_first = grown_first + jnp.where(first == 8 * j, growth[j], 0.0)
        grown_second = grown_second + jnp.where(second == j, growth[j], 0.0)
    sheet = jnp.concatenate([products, grown_first, grown_second] + [blank] * 5, axis=0)
    for target in range(groups):
        sent_ref[target] = sheet


def combine_kernel(z_ref, kept_ref, scalars_ref, basis_ref, images_ref, moved_ref, sent_ref):
    sectors, _, size = scalars_ref.shape
    tiny = 1e-30

    def over(x):
        return jnp.sum(x, axis=0, keepdims=True)

    def whole(x):
        return jnp.sum(x, axis=1, keepdims=True)

    def earlier(x, count):
        return pltpu.roll(x, size - count, 1)

    def later(x, count):
        return pltpu.roll(x, count, 1)

    grown_first, grown_second = scalars_ref[:, 1, :], scalars_ref[:, 2, :]
    most_first = jnp.maximum(jnp.max(grown_first, axis=0, keepdims=True), tiny)
    most_second = jnp.maximum(jnp.max(grown_second, axis=0, keepdims=True), tiny)
    rate_first = grown_first / most_first
    rate_second = grown_second / most_second
    products = over(scalars_ref[:, 0, :] * rate_first * rate_second)
    lane = lax.broadcasted_iota(jnp.int32, (1, size), 1)
    first, second = jnp.bitwise_and(lane, 56), jnp.bitwise_and(lane, 7)
    ratio_first = jnp.where(first < 8 * ITERS, earlier(most_first, 8) / most_first, 0.0)
    ratio_second = jnp.where(second < ITERS, earlier(most_second, 1) / most_second, 0.0)
    gram = jnp.where(lane < 64, products, 0.0)
    held = jnp.where(lane < 64, 0.0, products)
    on_energy = ratio_second * earlier(gram, 1)
    on_scale = ratio_first * ratio_second * earlier(gram, 9)
    vector_first = jnp.where(first == 0, 1.0, 0.0)
    vector_second = jnp.where(second == 0, 1.0, 0.0)
    square = whole(gram * vector_first * vector_second)
    for step in range(ITERS):
        weights = vector_first * vector_second
        energy = whole(weights * on_energy)
        image_square = whole(weights * on_scale)
        rate = step_size / jnp.sqrt(image_square + norm_eps)
        keep = 1.0 + rate * energy
        update_square = keep * (keep * square - 2.0 * rate * energy) + rate * rate * image_square
        shrink = 1.0 / jnp.sqrt(update_square + norm_eps)
        keep, rate = keep * shrink, rate * shrink
        square = update_square * (shrink * shrink)
        vector_first = keep * vector_first - rate * later(ratio_first * vector_first, 8)
        vector_second = keep * vector_second - rate * later(ratio_second * vector_second, 1)
    masked = whole(held * vector_first * vector_second)
    shrink = 1.0 / jnp.sqrt(jnp.maximum(masked, 0.0) + norm_eps)
    mine = lax.broadcasted_iota(jnp.int32, (sectors, size), 0) == z_ref[0]
    factors = over(jnp.where(mine, rate_first, 0.0)) * vector_first * shrink
    result = jnp.zeros((size, size), jnp.float32)
    moved = jnp.zeros((size, size), jnp.float32)
    for j in range(ITERS + 1):
        factor = factors[:, 8 * j:8 * j + 1]
        result = result + factor * basis_ref[j]
        moved = moved + factor * images_ref[j]
    columns = lax.broadcasted_iota(jnp.int32, (size, size), 1)
    held = columns < kept_ref[0, z_ref[0]]
    result = jnp.where(held, result, 0.0)
    moved = jnp.where(held, moved, 0.0)
    moved_ref[...] = moved
    for target in range(sectors):
        sent_ref[target, 0] = result


def fill_kernel(moved_ref, _, sent_ref):
    for target in range(sent_ref.shape[0]):
        sent_ref[target, 1] = moved_ref[...]


def stage_kernel(left_ref, out_ref):
    own, sectors, _, _ = left_ref.shape
    for term in range(own):
        for sector in range(sectors):
            out_ref[term, sector] = left_operand(left_ref[term, sector])


def boundary_kernel(shared_ref, left_ref, psi_ref, out_ref, made_ref, sems):
    own, sectors, size, _ = left_ref.shape
    copies = []
    for sector in range(sectors):
        at = LAST.index(FIRST[sector])
        copies.append(pltpu.make_async_copy(shared_ref.at[at, 0], psi_ref.at[0, sector], sems.at[sector]))
        copies[-1].start()
    for sector in range(sectors):
        u = shared_ref[LAST.index(FIRST[sector]), 1]
        right = right_operand(u)
        across = left_operand(u.T)
        for term in range(own):
            half = mm(left_ref[term, sector], right)
            half = half[:, :size] + half[:, size:]
            made_ref[sector, term] = joined(across, half)
        copies.append(pltpu.make_async_copy(made_ref.at[sector], out_ref.at[0, :, sector], sems.at[sectors + sector]))
        copies[-1].start()
    for copy in copies:
        copy.wait()


def vmem():
    return pl.BlockSpec(memory_space=pltpu.VMEM)


def smem():
    return pl.BlockSpec(memory_space=pltpu.SMEM)


def call(kernel, out_shape, in_specs, flops, scratch=(), aliases={}, out_spec=pl.BlockSpec(memory_space=pltpu.VMEM)):
    return pl.pallas_call(
        kernel,
        out_shape=out_shape,
        in_specs=in_specs,
        out_specs=jax.tree.map(lambda _: out_spec, out_shape),
        scratch_shapes=scratch,
        input_output_aliases=aliases,
        compiler_params=pltpu.CompilerParams(vmem_limit_bytes=VMEM_LIMIT),
        cost_estimate=pl.CostEstimate(flops=flops, bytes_accessed=4 << 20, transcendentals=0),
    )


def struct(*shape):
    return jax.ShapeDtypeStruct(shape, jnp.float32)


def product(a, b):
    return jnp.dot(a, b, precision=lax.Precision.HIGHEST, preferred_element_type=jnp.float32)


def scanned(own):
    whole = own
    prefix = None
    for level, axis in enumerate(SCAN):
        with jax.named_scope("scan_" + axis):
            pair = lax.all_gather(whole, axis)
            upper = lax.axis_index(axis) == 1
            if prefix is None:
                prefix = jnp.where(upper, pair[0], jnp.eye(own.shape[0], dtype=own.dtype))
            else:
                prefix = jnp.where(upper, product(pair[0], prefix), prefix)
            if level + 1 < len(SCAN):
                whole = product(pair[0], pair[1])
    return prefix


def per_device(left_env, right_env, transfer, psi_start, kept):
    left, right, transfer, psi = left_env[0], right_env[0], transfer[0], psi_start[0]
    own, sectors, size, _ = left.shape
    z = lax.axis_index(TERM)
    z = jnp.bitwise_and(jnp.right_shift(jnp.int32(OWNERS), 4 * z), 7)
    spot = z[None]
    pairs = [(source, source + 1) for source in range(63)]
    with jax.named_scope("gather_terms"):
        outgoing = jnp.concatenate([left, right], axis=0)
        blocks = lax.all_to_all(outgoing, TERM, 1, 0, axis_index_groups=[list(FIRST)], tiled=False)
    with jax.named_scope("prefix"):
        prefix = scanned(lax.dynamic_index_in_dim(transfer, z, 0, keepdims=False))
    with jax.named_scope("left_previous"):
        late, _ = lax.optimization_barrier((left, prefix))
        left_previous = lax.ppermute(late, SITE, pairs)
    with jax.named_scope("prepare"):
        operand = jax.ShapeDtypeStruct((size, 2 * size), jnp.bfloat16)
        ready = call(
            prepare_kernel,
            (struct(size, size), struct(size, size), operand, operand),
            [smem(), vmem(), vmem()],
            20 * size**3,
        )(spot, prefix, psi)
    with jax.named_scope("krylov"):
        terms = own * sectors
        basis, images, sent = call(
            krylov_kernel,
            (struct(ITERS + 1, size, size), struct(ITERS + 1, size, size), struct(sectors, 8, size)),
            [smem(), smem()] + [vmem()] * 5,
            ITERS * terms * 4 * 2 * 3 * size**3,
            [pltpu.VMEM((terms * size, 2 * size), jnp.bfloat16)] * 2,
        )(spot, kept, blocks, *ready)
    with jax.named_scope("share_scalars"):
        scalars = lax.all_to_all(sent, TERM, 0, 0, axis_index_groups=[list(FIRST)], tiled=True)
    with jax.named_scope("combine"):
        moved, sent = call(
            combine_kernel,
            (struct(size, size), struct(sectors, 2, size, size)),
            [smem(), smem()] + [vmem()] * 3,
            size**2 * 100,
        )(spot, kept, scalars, basis, images)
    with jax.named_scope("hand_on"):
        moved, left_previous = lax.optimization_barrier((moved, left_previous))
        moved = lax.ppermute(moved, SITE, pairs)
        staged = call(
            stage_kernel,
            jax.ShapeDtypeStruct((own, sectors, size, 2 * size), jnp.bfloat16),
            [vmem()],
            own * sectors * size**3,
        )(left_previous)
        moved, staged = lax.optimization_barrier((moved, staged))
    with jax.named_scope("share"):
        sent = call(
            fill_kernel,
            struct(sectors, 2, size, size),
            [vmem(), vmem()],
            size**2,
            aliases={1: 0},
        )(moved, sent)
        shared = lax.all_to_all(sent, TERM, 0, 0, axis_index_groups=[list(LAST)], tiled=True)
    with jax.named_scope("boundary"):
        result, incoming = call(
            boundary_kernel,
            (struct(1, sectors, size, size), struct(1, own, sectors, size, size)),
            [vmem(), vmem()],
            own * sectors * 12 * size**3,
            [pltpu.VMEM((sectors, own, size, size), jnp.float32), pltpu.SemaphoreType.DMA((2 * sectors,))],
            out_spec=pl.BlockSpec(memory_space=pl.ANY),
        )(shared, staged)
    return result, incoming


def solution(mesh):
    fine = Mesh(mesh.devices.reshape((2,) * 6 + (8,)), SITE + (TERM,))
    placed = (
        P(SITE, TERM, None, None, None),
        P(SITE, TERM, None, None, None),
        P(SITE, None, None, None),
        P(SITE, None, None, None),
        P(SITE, None),
    )
    return jax.shard_map(
        per_device,
        mesh=fine,
        in_specs=placed,
        out_specs=(P(SITE, None, None, None), P(SITE, TERM, None, None, None)),
        check_vma=False,
    )
```

```python
import jax
import jax.numpy as jnp
from jax import lax
from jax.experimental import pallas as pl
from jax.experimental.pallas import tpu as pltpu
from jax.sharding import Mesh, PartitionSpec as P

ITERS = 4
norm_eps = 1e-06
step_size = 0.5
SITE = ("y2", "y1", "y0", "x1", "x0", "c")
SCAN = ("c", "x0", "x1", "y0", "y1", "y2")
TERM = "z"
FIRST = (0, 4, 1, 5, 2, 6, 3, 7)
OWNERS = sum(place << (4 * at) for place, at in enumerate(FIRST))
LAST = (7, 6, 5, 4, 3, 2, 1, 0)
VMEM_LIMIT = 24 * 1024 * 1024


def halves(x):
    high = x.astype(jnp.bfloat16)
    low = (x - high.astype(jnp.float32)).astype(jnp.bfloat16)
    return high, low


def mm(a, b):
    return jnp.dot(a, b, preferred_element_type=jnp.float32)


def left_operand(a):
    return jnp.concatenate(halves(a), axis=1)


def right_operand(b):
    high, low = halves(b)
    top = jnp.concatenate([high, low], axis=1)
    return jnp.concatenate([top, top], axis=0)


def joined(a, b):
    both = mm(a, right_operand(b))
    size = b.shape[1]
    return both[:, :size] + both[:, size:]


def total(x):
    return jnp.sum(jnp.sum(x, axis=0, keepdims=True), axis=1, keepdims=True)


def prepare_kernel(z_ref, prefix_ref, start_ref, x_ref, w_ref, backward_ref, square_ref):
    sectors, size, _ = start_ref.shape
    prefix = prefix_ref[...]
    forward = left_operand(prefix)
    backward_ref[...] = left_operand(prefix.T)
    square_ref[...] = left_operand(joined(forward, prefix.T))
    squares = jnp.zeros((size, size), jnp.float32)
    for sector in range(sectors):
        squares = squares + start_ref[sector] * start_ref[sector]
    x = start_ref[z_ref[0]] / jnp.sqrt(total(squares) + norm_eps)
    x_ref[...] = x
    w_ref[...] = joined(forward, x)


def krylov_kernel(z_ref, kept_ref, blocks_ref, x_ref, w_ref, backward_ref, square_ref, basis_ref, moved_ref, sent_ref, left_ref, right_ref):
    groups, per_group, size, _ = blocks_ref.shape
    own = per_group // 2
    terms = groups * own
    x, w = x_ref[...], w_ref[...]
    backward, square = backward_ref[...], square_ref[...]
    for group in range(groups):
        for term in range(own):
            at = (group * own + term) * size
            left_ref[at:at + size, :] = left_operand(blocks_ref[group, term])
            high, low = halves(blocks_ref[group, own + term])
            right_ref[at:at + size, :] = jnp.concatenate([high, low], axis=1)
    basis_ref[0] = x
    moved_ref[0] = w
    images = []
    growth = [jnp.ones((1, 1), jnp.float32)]
    for step in range(ITERS):
        middle = joined(left_ref[...], w)
        high, low = halves(middle)
        wide = jnp.concatenate(
            [
                jnp.concatenate([part[t * size:(t + 1) * size] for t in range(terms)], axis=1)
                for part in (high, low)
            ],
            axis=0,
        )
        both = mm(wide, right_ref[...])
        y = (both[:size, :size] + both[size:, size:]) + (both[:size, size:] + both[size:, :size])
        length = jnp.sqrt(total(y * y))
        shrink = jnp.where(length > 0.0, 1.0 / length, 0.0)
        w = joined(square, y) * shrink
        moved_ref[step + 1] = w
        images.append(y * shrink)
        growth.append(growth[step] * length)
    later = joined(backward, jnp.concatenate(images, axis=1))
    basis = [x] + [later[:, step * size:(step + 1) * size] for step in range(ITERS)]
    for step in range(ITERS):
        basis_ref[step + 1] = basis[step + 1]
    blank = jnp.zeros((1, size), jnp.float32)
    across = {}
    for i in range(ITERS + 1):
        for j in range(i, ITERS + 1):
            across[i, j] = across[j, i] = jnp.sum(basis[i] * basis[j], axis=0, keepdims=True)
    across = jnp.concatenate([across.get((i, j), blank) for i in range(8) for j in range(8)], axis=0)
    columns = lax.broadcasted_iota(jnp.int32, (64, size), 1)
    place = lax.broadcasted_iota(jnp.int32, (64, size), 0)
    held = columns < kept_ref[0, z_ref[0]]
    full = jnp.sum(across, axis=1, keepdims=True)
    held = jnp.sum(jnp.where(held, across, 0.0), axis=1, keepdims=True)
    placed = jnp.where(columns == place, full, 0.0) + jnp.where(columns == place + 64, held, 0.0)
    products = jnp.sum(placed, axis=0, keepdims=True)
    lane = lax.broadcasted_iota(jnp.int32, (1, size), 1)
    first, second = jnp.bitwise_and(lane, 56), jnp.bitwise_and(lane, 7)
    grown_first, grown_second = blank, blank
    for j in range(ITERS + 1):
        grown_first = grown_first + jnp.where(first == 8 * j, growth[j], 0.0)
        grown_second = grown_second + jnp.where(second == j, growth[j], 0.0)
    sheet = jnp.concatenate([products, grown_first, grown_second] + [blank] * 5, axis=0)
    for target in range(groups):
        sent_ref[target] = sheet


def combine_kernel(z_ref, kept_ref, scalars_ref, basis_ref, images_ref, moved_ref, psi_ref):
    sectors, _, size = scalars_ref.shape
    tiny = 1e-30

    def over(x):
        return jnp.sum(x, axis=0, keepdims=True)

    def whole(x):
        return jnp.sum(x, axis=1, keepdims=True)

    def earlier(x, count):
        return pltpu.roll(x, size - count, 1)

    def later(x, count):
        return pltpu.roll(x, count, 1)

    grown_first, grown_second = scalars_ref[:, 1, :], scalars_ref[:, 2, :]
    most_first = jnp.maximum(jnp.max(grown_first, axis=0, keepdims=True), tiny)
    most_second = jnp.maximum(jnp.max(grown_second, axis=0, keepdims=True), tiny)
    rate_first = grown_first / most_first
    rate_second = grown_second / most_second
    products = over(scalars_ref[:, 0, :] * rate_first * rate_second)
    lane = lax.broadcasted_iota(jnp.int32, (1, size), 1)
    first, second = jnp.bitwise_and(lane, 56), jnp.bitwise_and(lane, 7)
    ratio_first = jnp.where(first < 8 * ITERS, earlier(most_first, 8) / most_first, 0.0)
    ratio_second = jnp.where(second < ITERS, earlier(most_second, 1) / most_second, 0.0)
    gram = jnp.where(lane < 64, products, 0.0)
    held = jnp.where(lane < 64, 0.0, products)
    on_energy = ratio_second * earlier(gram, 1)
    on_scale = ratio_first * ratio_second * earlier(gram, 9)
    vector_first = jnp.where(first == 0, 1.0, 0.0)
    vector_second = jnp.where(second == 0, 1.0, 0.0)
    square = whole(gram * vector_first * vector_second)
    for step in range(ITERS):
        weights = vector_first * vector_second
        energy = whole(weights * on_energy)
        image_square = whole(weights * on_scale)
        rate = step_size / jnp.sqrt(image_square + norm_eps)
        keep = 1.0 + rate * energy
        update_square = keep * (keep * square - 2.0 * rate * energy) + rate * rate * image_square
        shrink = 1.0 / jnp.sqrt(update_square + norm_eps)
        keep, rate = keep * shrink, rate * shrink
        square = update_square * (shrink * shrink)
        vector_first = keep * vector_first - rate * later(ratio_first * vector_first, 8)
        vector_second = keep * vector_second - rate * later(ratio_second * vector_second, 1)
    masked = whole(held * vector_first * vector_second)
    shrink = 1.0 / jnp.sqrt(jnp.maximum(masked, 0.0) + norm_eps)
    mine = lax.broadcasted_iota(jnp.int32, (sectors, size), 0) == z_ref[0]
    factors = over(jnp.where(mine, rate_first, 0.0)) * vector_first * shrink
    result = jnp.zeros((size, size), jnp.float32)
    moved = jnp.zeros((size, size), jnp.float32)
    for j in range(ITERS + 1):
        factor = factors[:, 8 * j:8 * j + 1]
        result = result + factor * basis_ref[j]
        moved = moved + factor * images_ref[j]
    columns = lax.broadcasted_iota(jnp.int32, (size, size), 1)
    held = columns < kept_ref[0, z_ref[0]]
    result = jnp.where(held, result, 0.0)
    moved = jnp.where(held, moved, 0.0)
    moved_ref[...] = moved
    psi_ref[...] = result


def fill_kernel(moved_ref, _, sent_ref):
    for target in range(sent_ref.shape[0]):
        sent_ref[target, 1] = moved_ref[...]


def stage_kernel(left_ref, psi_ref, out_ref, sent_ref):
    own, sectors, _, _ = left_ref.shape
    for target in range(sectors):
        sent_ref[target, 0] = psi_ref[...]
    for term in range(own):
        for sector in range(sectors):
            out_ref[term, sector] = left_operand(left_ref[term, sector])


def boundary_kernel(shared_ref, left_ref, psi_ref, out_ref, made_ref, sems):
    own, sectors, size, _ = left_ref.shape
    copies = []
    for sector in range(sectors):
        at = LAST.index(FIRST[sector])
        copies.append(pltpu.make_async_copy(shared_ref.at[at, 0], psi_ref.at[0, sector], sems.at[sector]))
        copies[-1].start()
    for sector in range(sectors):
        u = shared_ref[LAST.index(FIRST[sector]), 1]
        right = right_operand(u)
        across = left_operand(u.T)
        for term in range(own):
            half = mm(left_ref[term, sector], right)
            half = half[:, :size] + half[:, size:]
            made_ref[sector, term] = joined(across, half)
        copies.append(pltpu.make_async_copy(made_ref.at[sector], out_ref.at[0, :, sector], sems.at[sectors + sector]))
        copies[-1].start()
    for copy in copies:
        copy.wait()


def vmem():
    return pl.BlockSpec(memory_space=pltpu.VMEM)


def smem():
    return pl.BlockSpec(memory_space=pltpu.SMEM)


def call(kernel, out_shape, in_specs, flops, scratch=(), aliases={}, out_spec=pl.BlockSpec(memory_space=pltpu.VMEM)):
    return pl.pallas_call(
        kernel,
        out_shape=out_shape,
        in_specs=in_specs,
        out_specs=jax.tree.map(lambda _: out_spec, out_shape),
        scratch_shapes=scratch,
        input_output_aliases=aliases,
        compiler_params=pltpu.CompilerParams(vmem_limit_bytes=VMEM_LIMIT),
        cost_estimate=pl.CostEstimate(flops=flops, bytes_accessed=4 << 20, transcendentals=0),
    )


def struct(*shape):
    return jax.ShapeDtypeStruct(shape, jnp.float32)


def product(a, b):
    return jnp.dot(a, b, precision=lax.Precision.HIGHEST, preferred_element_type=jnp.float32)


def scanned(own):
    whole = own
    prefix = None
    for level, axis in enumerate(SCAN):
        with jax.named_scope("scan_" + axis):
            pair = lax.all_gather(whole, axis)
            upper = lax.axis_index(axis) == 1
            if prefix is None:
                prefix = jnp.where(upper, pair[0], jnp.eye(own.shape[0], dtype=own.dtype))
            else:
                prefix = jnp.where(upper, product(pair[0], prefix), prefix)
            if level + 1 < len(SCAN):
                whole = product(pair[0], pair[1])
    return prefix


def per_device(left_env, right_env, transfer, psi_start, kept):
    left, right, transfer, psi = left_env[0], right_env[0], transfer[0], psi_start[0]
    own, sectors, size, _ = left.shape
    z = lax.axis_index(TERM)
    z = jnp.bitwise_and(jnp.right_shift(jnp.int32(OWNERS), 4 * z), 7)
    spot = z[None]
    pairs = [(source, source + 1) for source in range(63)]
    with jax.named_scope("gather_terms"):
        outgoing = jnp.stack([part[term] for part in (left, right) for term in range(own)], axis=1)
        blocks = lax.all_to_all(outgoing, TERM, 0, 0, axis_index_groups=[list(FIRST)], tiled=True)
    with jax.named_scope("prefix"):
        prefix = scanned(lax.dynamic_index_in_dim(transfer, z, 0, keepdims=False))
    with jax.named_scope("left_previous"):
        late, _ = lax.optimization_barrier((left, prefix))
        left_previous = lax.ppermute(late, SITE, pairs)
    with jax.named_scope("prepare"):
        operand = jax.ShapeDtypeStruct((size, 2 * size), jnp.bfloat16)
        ready = call(
            prepare_kernel,
            (struct(size, size), struct(size, size), operand, operand),
            [smem(), vmem(), vmem()],
            20 * size**3,
        )(spot, prefix, psi)
    with jax.named_scope("krylov"):
        terms = own * sectors
        basis, images, sent = call(
            krylov_kernel,
            (struct(ITERS + 1, size, size), struct(ITERS + 1, size, size), struct(sectors, 8, size)),
            [smem(), smem()] + [vmem()] * 5,
            ITERS * terms * 4 * 2 * 3 * size**3,
            [pltpu.VMEM((terms * size, 2 * size), jnp.bfloat16)] * 2,
        )(spot, kept, blocks, *ready)
    with jax.named_scope("share_scalars"):
        scalars = lax.all_to_all(sent, TERM, 0, 0, axis_index_groups=[list(FIRST)], tiled=True)
    with jax.named_scope("combine"):
        moved, result = call(
            combine_kernel,
            (struct(size, size), struct(size, size)),
            [smem(), smem()] + [vmem()] * 3,
            size**2 * 100,
        )(spot, kept, scalars, basis, images)
    with jax.named_scope("hand_on"):
        moved, left_previous = lax.optimization_barrier((moved, left_previous))
        moved = lax.ppermute(moved, SITE, pairs)
        staged, sent = call(
            stage_kernel,
            (jax.ShapeDtypeStruct((own, sectors, size, 2 * size), jnp.bfloat16), struct(sectors, 2, size, size)),
            [vmem(), vmem()],
            own * sectors * size**3,
        )(left_previous, result)
        moved, staged = lax.optimization_barrier((moved, staged))
    with jax.named_scope("share"):
        sent = call(
            fill_kernel,
            struct(sectors, 2, size, size),
            [vmem(), vmem()],
            size**2,
            aliases={1: 0},
        )(moved, sent)
        shared = lax.all_to_all(sent, TERM, 0, 0, axis_index_groups=[list(LAST)], tiled=True)
    with jax.named_scope("boundary"):
        result, incoming = call(
            boundary_kernel,
            (struct(1, sectors, size, size), struct(1, own, sectors, size, size)),
            [vmem(), vmem()],
            own * sectors * 12 * size**3,
            [pltpu.VMEM((sectors, own, size, size), jnp.float32), pltpu.SemaphoreType.DMA((2 * sectors,))],
            out_spec=pl.BlockSpec(memory_space=pl.ANY),
        )(shared, staged)
    return result, incoming


def solution(mesh):
    fine = Mesh(mesh.devices.reshape((2,) * 6 + (8,)), SITE + (TERM,))
    placed = (
        P(SITE, TERM, None, None, None),
        P(SITE, TERM, None, None, None),
        P(SITE, None, None, None),
        P(SITE, None, None, None),
        P(SITE, None),
    )
    return jax.shard_map(
        per_device,
        mesh=fine,
        in_specs=placed,
        out_specs=(P(SITE, None, None, None), P(SITE, TERM, None, None, None)),
        check_vma=False,
    )
```
